32 devices in a mesh: dp: 4 (over y, core), ctx: 8 (over z, x).
Axes of the slice: x: 2, y: 2, z: 4, core: 2. Of those that a mesh axis runs over, the one named last changes fastest.
Arguments:
- queries: bfloat16 [4, 2048, 2560], P('dp', 'ctx'), may hold values from -120 to 120
- global_keys: bfloat16 [4, 2048, 512], P('dp', 'ctx'), may hold values from -5 to 5
- global_values: bfloat16 [4, 2048, 512], P('dp', 'ctx'), may hold values from -6 to 6
- out_grad: bfloat16 [4, 2048, 2560], P('dp', 'ctx'), may hold values from -6 to 6
- query_gain: float32 [2560], replicated, may hold values from 0.5 to 1.5
- doc_start: int32 [4, 16], P('dp', 'ctx'), may hold values from 0 to 15, as said below
Outputs:
- attn_out: bfloat16 [4, 2048, 2560], P('dp', 'ctx')
- query_grad: bfloat16 [4, 2048, 2560], P('dp', 'ctx')
- key_grad: bfloat16 [4, 2048, 512], P('dp', 'ctx')
- value_grad: bfloat16 [4, 2048, 512], P('dp', 'ctx')
- gain_grad: float32 [2560], replicated
The draws below stay inside these ranges and needn't reach their ends.
Inputs may be any that keep to these rules, and one draw needn't show every extreme that they name: doc_start[g, b] is the first block of block b's document: it is at most b and at least b - 6, never falls along b, and equals b where a document begins; every slab has a document of exactly 7 blocks.
All inputs are finite; a program needn't handle non-finite values.
Results may differ from the reference program's by a relative error of at most 0.017.
The reference program's roundings to bfloat16 on the way count: a program that leaves them out, or rounds other values in their place, can miss the bound.
Values may be sent and summed in bfloat16 or wider, within the bound.
A program may use at most 64 MiB of HBM per device.

```python
import math
import jax
import jax.numpy as jnp
from jax import lax

HEADS = 20
KV_HEADS = 4
HD = 128
BLOCK = 128
REACH = 4
TOK_DEV = 256
GROUPS = 4
SEQ = 2048
DOC_BLOCKS = 7
N_CTX = 8


def shared_keys(key):
    raw = jax.random.normal(jax.random.fold_in(key, 7), (GROUPS, SEQ, KV_HEADS * HD), jnp.float32)
    return jnp.clip(raw, -5.0, 5.0)


def draw_global_keys(key, part):
    base = shared_keys(key)
    return base.astype(jnp.bfloat16)


def draw_queries(key, part):
    drawn = jax.random.normal(jax.random.fold_in(key, 13), (GROUPS, SEQ, HEADS * HD), jnp.float32)
    drawn = jnp.clip(drawn, -5.0, 5.0)
    return drawn.astype(jnp.bfloat16)


def draw_doc_start(key, part):
    count = SEQ // BLOCK

    def one_group(group_key):
        lengths = jax.random.randint(jax.random.fold_in(group_key, 1), (count,), 1, DOC_BLOCKS + 1)
        longest = jax.random.randint(jax.random.fold_in(group_key, 2), (), 0, count // DOC_BLOCKS)
        lengths = jnp.where(jnp.arange(count) == longest, DOC_BLOCKS, lengths)
        starts = jnp.cumsum(lengths) - lengths
        blocks = jnp.arange(count)
        return jnp.max(jnp.where(starts[None, :] <= blocks[:, None], starts[None, :], 0), axis=1)
    group_keys = jax.vmap(lambda index: jax.random.fold_in(key, index))(jnp.arange(GROUPS))
    return jax.vmap(one_group)(group_keys).astype(jnp.int32)


def levels(own_key, dims, split, smallest, top_value):
    factor_of = 1.0
    for position, shards_of in split:
        heights = jax.random.uniform(jax.random.fold_in(jax.random.fold_in(own_key, 6), position), (shards_of,), jnp.float32, smallest / len(split), top_value / len(split))
        factor_of = factor_of * jnp.repeat(jnp.exp(heights), dims[position] // shards_of).reshape((-1,) + (1,) * (len(dims) - 1 - position))
    return factor_of


def centred(key, shape, scale, bound, shards=(), held_as=jnp.bfloat16):
    values = scale * jax.random.normal(key, shape, jnp.float32)
    if shards:
        values = values * levels(key, shape, shards, -0.22, 0.18)
    return jnp.clip(values, -bound, bound).astype(held_as)


def setup_inputs(seed: int = 0) -> dict:
    key_of = jax.random.split(jax.random.key(seed), 7)
    queries = draw_queries(jax.random.fold_in(key_of[6], 71), 0)
    global_keys = draw_global_keys(jax.random.fold_in(key_of[6], 71), 0)
    global_values = centred(key_of[2], (GROUPS, SEQ, KV_HEADS * HD), 1.0, 6.0, ((0, 4), (1, 8)))
    out_grad = centred(key_of[3], (GROUPS, SEQ, HEADS * HD), 1.0, 6.0, ((0, 4), (1, 8)))
    query_gain = jnp.clip(1.0 + 0.1 * jax.random.normal(key_of[4], (HEADS * HD,), jnp.float32), 0.5, 1.5)
    doc_start = draw_doc_start(jax.random.fold_in(key_of[6], 71), 0)
    return {"queries": queries, "global_keys": global_keys, "global_values": global_values, "out_grad": out_grad, "query_gain": query_gain, "doc_start": doc_start}


def core_block(query_block, key_window, value_window, grad_block, allowed):
    kv_count = key_window.shape[1] // HD
    group_size = query_block.shape[1] // (kv_count * HD)
    factor = 1.0 / math.sqrt(HD)
    query_four = query_block.astype(jnp.float32).reshape(query_block.shape[0], kv_count, group_size, HD)
    grad_four = grad_block.astype(jnp.float32).reshape(grad_block.shape[0], kv_count, group_size, HD)
    key_three = key_window.astype(jnp.float32).reshape(key_window.shape[0], kv_count, HD)
    value_three = value_window.astype(jnp.float32).reshape(value_window.shape[0], kv_count, HD)
    scores = jnp.einsum('tcgd,wcd->cgtw', query_four, key_three) * factor
    scores = jnp.where(allowed[None, None], scores, -jnp.inf)
    row_max = lax.optimization_barrier(jnp.max(scores, axis=-1, keepdims=True))
    log_total = row_max + jnp.log(lax.optimization_barrier(jnp.sum(jnp.exp(scores - row_max), axis=-1, keepdims=True)))
    weights = jnp.exp(scores - log_total)
    weights_low = weights.astype(jnp.bfloat16).astype(jnp.float32)
    result = jnp.einsum('cgtw,wcd->tcgd', weights_low, value_three).astype(jnp.bfloat16)
    inner_sum = lax.optimization_barrier(jnp.sum(grad_four * result.astype(jnp.float32), axis=-1))
    inner_sum = jnp.transpose(inner_sum, (1, 2, 0))
    dweights = jnp.einsum('tcgd,wcd->cgtw', grad_four, value_three)
    dscore = weights * (dweights - inner_sum[..., None])
    dscore_low = dscore.astype(jnp.bfloat16).astype(jnp.float32)
    dquery = jnp.einsum('cgtw,wcd->tcgd', dscore_low, key_three) * factor
    dkey = jnp.einsum('cgtw,tcgd->wcd', dscore_low, query_four) * factor
    dvalue = jnp.einsum('cgtw,tcgd->wcd', weights_low, grad_four)
    row_count = query_block.shape[0]
    width = key_window.shape[0]
    return (result.reshape(row_count, -1), dquery.reshape(row_count, -1), dkey.reshape(width, -1), dvalue.reshape(width, -1))

def one_slab(inputs, query_gain):
    queries, global_keys, global_values, out_grad, doc_start = inputs
    scaled = (queries.astype(jnp.float32) * query_gain).astype(jnp.bfloat16)
    width = REACH * TOK_DEV
    lead_rows = (REACH - 1) * TOK_DEV
    channels = global_keys.shape[1]
    padded_keys = jnp.concatenate([jnp.zeros((lead_rows, channels), jnp.bfloat16), global_keys], axis=0)
    padded_values = jnp.concatenate([jnp.zeros((lead_rows, channels), jnp.bfloat16), global_values], axis=0)
    begins = jnp.repeat(doc_start, BLOCK).astype(jnp.int32) * BLOCK

    def step(carry, device):
        key_acc, value_acc = carry
        base = (device * TOK_DEV).astype(jnp.int32)
        query_block = lax.dynamic_slice_in_dim(scaled, base, TOK_DEV, 0)
        grad_block = lax.dynamic_slice_in_dim(out_grad, base, TOK_DEV, 0)
        key_window = lax.dynamic_slice_in_dim(padded_keys, base, width, 0)
        value_window = lax.dynamic_slice_in_dim(padded_values, base, width, 0)
        query_pos = base + jnp.arange(TOK_DEV, dtype=jnp.int32)
        key_pos = base - lead_rows + jnp.arange(width, dtype=jnp.int32)
        first = lax.dynamic_slice_in_dim(begins, base, TOK_DEV, 0)
        allowed = (key_pos[None, :] <= query_pos[:, None]) & (key_pos[None, :] >= first[:, None])
        result, dquery, dkey, dvalue = core_block(query_block, key_window, value_window, grad_block, allowed)
        key_acc = lax.dynamic_update_slice_in_dim(key_acc, lax.dynamic_slice_in_dim(key_acc, base, width, 0) + dkey, base, 0)
        value_acc = lax.dynamic_update_slice_in_dim(value_acc, lax.dynamic_slice_in_dim(value_acc, base, width, 0) + dvalue, base, 0)
        return ((key_acc, value_acc), (result, dquery))
    start_acc = jnp.zeros((lead_rows + SEQ, channels), jnp.float32)
    (key_acc, value_acc), (results, dqueries) = lax.scan(step, (start_acc, start_acc), jnp.arange(N_CTX, dtype=jnp.int32))
    attn_out = results.reshape(SEQ, -1)
    dscaled = dqueries.reshape(SEQ, -1)
    query_grad = (dscaled * query_gain).astype(jnp.bfloat16)
    gain_term = lax.optimization_barrier(jnp.sum(dscaled * queries.astype(jnp.float32), axis=0))
    return (attn_out, query_grad, key_acc[lead_rows:].astype(jnp.bfloat16), value_acc[lead_rows:].astype(jnp.bfloat16), gain_term)

def reference(queries, global_keys, global_values, out_grad, query_gain, doc_start):
    attn_out, query_grad, key_grad, value_grad, gain_terms = lax.map(lambda inputs: one_slab(inputs, query_gain), (queries, global_keys, global_values, out_grad, doc_start))
    return (attn_out, query_grad, key_grad, value_grad, lax.optimization_barrier(jnp.sum(gain_terms, axis=0)))
```

```python
import functools
import math

import jax
import jax.numpy as jnp
from jax import lax
from jax.experimental import pallas as pl
from jax.experimental.pallas import tpu as pltpu
from jax.sharding import PartitionSpec as P

HD = 128
BLOCK = 128
REACH = 4
FAR = REACH - 1
NEG = -1e30
MESH = pl.DeviceIdType.MESH


def nt(left, right):
    return lax.dot_general(left, right, (((1,), (1,)), ((), ())), preferred_element_type=jnp.float32)


def nn(left, right):
    return jnp.dot(left, right, preferred_element_type=jnp.float32)


def kernel(
    n_dp,
    n_ctx,
    q_hbm,
    k_hbm,
    v_hbm,
    g_hbm,
    gain_ref,
    begins_ref,
    out_hbm,
    dq_hbm,
    dk_hbm,
    dv_hbm,
    gain_out,
    q_buf,
    g_buf,
    kv_buf,
    tri,
    s_buf,
    dp_buf,
    p_all,
    ds_all,
    qs_all,
    k_t,
    v_t,
    part_out,
    part_in,
    part_own,
    out_buf,
    dq_buf,
    kv_out,
    term,
    term_ctx,
    total,
    total_dp,
    load_sem,
    own_sem,
    send_sem,
    recv_sem,
    psend_sem,
    precv_sem,
    store_sem,
    kvst_sem,
    csend_sem,
    crecv_sem,
    dsend_sem,
    drecv_sem,
):
    heads, rows, _ = q_buf.shape
    kv_count = kv_buf.shape[0]
    group = heads // kv_count
    width = REACH * rows
    dp = lax.axis_index("dp")
    me = lax.axis_index("ctx")
    factor = 1.0 / math.sqrt(HD)
    log2_factor = factor * math.log2(math.e)

    def cols(index):
        return pl.ds(pl.multiple_of(index * HD, HD), HD)

    def load_q(h):
        return pltpu.make_async_copy(q_hbm.at[0, :, cols(h)], q_buf.at[h], load_sem.at[0, h])

    def load_g(h):
        return pltpu.make_async_copy(g_hbm.at[0, :, cols(h)], g_buf.at[h], load_sem.at[1, h])

    def load_k(c):
        return pltpu.make_async_copy(k_hbm.at[0, :, cols(c)], kv_buf.at[c, 0, FAR], own_sem.at[0, c])

    def load_v(c):
        return pltpu.make_async_copy(v_hbm.at[0, :, cols(c)], kv_buf.at[c, 1, FAR], own_sem.at[1, c])

    def send_kv(c, dist, which):
        source = (k_hbm, v_hbm)[which]
        return pltpu.make_async_remote_copy(
            src_ref=source.at[0, :, cols(c)],
            dst_ref=kv_buf.at[c, which, FAR - dist],
            send_sem=send_sem.at[c, dist - 1, which],
            recv_sem=recv_sem.at[c, dist - 1, which],
            device_id={"ctx": lax.rem(me + dist, n_ctx)},
            device_id_type=MESH,
        )

    def send_part(c, dist):
        return pltpu.make_async_remote_copy(
            src_ref=part_out.at[c, dist - 1],
            dst_ref=part_in.at[c, dist - 1],
            send_sem=psend_sem.at[c, dist - 1],
            recv_sem=precv_sem.at[c, dist - 1],
            device_id={"ctx": lax.rem(me + n_ctx - dist, n_ctx)},
            device_id_type=MESH,
        )

    def store_out(h):
        return pltpu.make_async_copy(out_buf.at[h], out_hbm.at[0, :, cols(h)], store_sem.at[0, h])

    def store_dq(h):
        return pltpu.make_async_copy(dq_buf.at[h], dq_hbm.at[0, :, cols(h)], store_sem.at[1, h])

    def store_dk(c):
        return pltpu.make_async_copy(kv_out.at[c, 0], dk_hbm.at[0, :, cols(c)], kvst_sem.at[0, c])

    def store_dv(c):
        return pltpu.make_async_copy(kv_out.at[c, 1], dv_hbm.at[0, :, cols(c)], kvst_sem.at[1, c])

    def send_ctx(step):
        return pltpu.make_async_remote_copy(
            src_ref=term,
            dst_ref=term_ctx.at[me],
            send_sem=csend_sem.at[step],
            recv_sem=crecv_sem.at[me],
            device_id={"ctx": lax.rem(me + step, n_ctx)},
            device_id_type=MESH,
        )

    def recv_ctx(peer):
        return pltpu.make_async_remote_copy(
            src_ref=term,
            dst_ref=term_ctx.at[peer],
            send_sem=csend_sem.at[0],
            recv_sem=crecv_sem.at[peer],
            device_id={"ctx": peer},
            device_id_type=MESH,
        )

    def send_dp(step):
        return pltpu.make_async_remote_copy(
            src_ref=total,
            dst_ref=total_dp.at[dp],
            send_sem=dsend_sem.at[step],
            recv_sem=drecv_sem.at[dp],
            device_id={"dp": lax.rem(dp + step, n_dp)},
            device_id_type=MESH,
        )

    def recv_dp(peer):
        return pltpu.make_async_remote_copy(
            src_ref=total,
            dst_ref=total_dp.at[peer],
            send_sem=dsend_sem.at[0],
            recv_sem=drecv_sem.at[peer],
            device_id={"dp": peer},
            device_id_type=MESH,
        )

    def each(count, body, start=0):
        def step(i, carry):
            body(i)
            return carry

        lax.fori_loop(start, count, step, 0)

    barrier = pltpu.get_barrier_semaphore()

    def greet_ctx(step):
        pl.semaphore_signal(
            barrier, inc=1, device_id={"ctx": lax.rem(me + step, n_ctx)}, device_id_type=MESH
        )

    def greet_dp(step):
        pl.semaphore_signal(
            barrier, inc=1, device_id={"dp": lax.rem(dp + step, n_dp)}, device_id_type=MESH
        )

    each(n_ctx, greet_ctx, 1)
    each(n_dp, greet_dp, 1)

    def start_loads(c):
        load_k(c).start()
        load_v(c).start()
        each(group, lambda g: (load_q(c * group + g).start(), load_g(c * group + g).start()))

    each(kv_count, start_loads)

    for dist in range(1, REACH):

        @pl.when(me < dist)
        def _():
            kv_buf[:, :, FAR - dist] = jnp.zeros((kv_count, 2, rows, HD), jnp.bfloat16)

    query_pos = me * rows + lax.broadcasted_iota(jnp.int32, (1, rows), 1)
    begins = begins_ref[...]
    key_pos = me * rows + lax.broadcasted_iota(jnp.int32, (rows, rows), 0)
    tri[...] = jnp.where((key_pos <= query_pos) & (key_pos >= begins), 0.0, NEG)

    pl.semaphore_wait(barrier, n_ctx - 1 + n_dp - 1)

    def start_sends(c):
        for dist in range(1, REACH):

            @pl.when(me + dist < n_ctx)
            def _():
                send_kv(c, dist, 0).start()
                send_kv(c, dist, 1).start()

    each(kv_count, start_sends)

    far_blocks = FAR * rows // BLOCK
    shown = []
    for w in range(far_blocks):
        first = (me - FAR) * rows + w * BLOCK
        shown.append(begins <= first)

    def one_kv(c):
        load_k(c).wait()
        load_v(c).wait()
        for dist in range(1, REACH):

            @pl.when(me >= dist)
            def _():
                send_kv(c, dist, 0).wait_recv()
                send_kv(c, dist, 1).wait_recv()

        keys = kv_buf[c, 0].reshape(width, HD)
        values = kv_buf[c, 1].reshape(width, HD)
        k_t[...] = keys.astype(jnp.float32).T.astype(jnp.bfloat16)
        v_t[...] = values.astype(jnp.float32).T.astype(jnp.bfloat16)

        for g in range(group):
            h = c * group + g
            lanes = pl.ds(g * rows, rows)
            s_g = s_buf.at[g % 2]
            dp_g = dp_buf.at[g % 2]
            load_q(h).wait()
            load_g(h).wait()
            gain = gain_ref[pl.ds(h, 1), :]
            raw = q_buf[h].astype(jnp.float32)
            query = (raw * gain).astype(jnp.bfloat16)
            qs_all[lanes, :] = query
            grad = g_buf[h]
            s_g[...] = nt(kv_buf[c, 0].reshape(width, HD), query)
            dp_g[...] = nt(kv_buf[c, 1].reshape(width, HD), grad)
            near = s_g[FAR * rows :, :] + tri[...]
            s_g[FAR * rows :, :] = near
            top = jnp.max(near, axis=0, keepdims=True)
            for w in range(far_blocks):
                block_top = jnp.max(s_g[w * BLOCK : (w + 1) * BLOCK, :], axis=0, keepdims=True)
                top = jnp.maximum(top, jnp.where(shown[w], block_top, NEG))
            top = top * log2_factor
            norm = jnp.zeros((1, rows), jnp.float32)
            for w in range(width // BLOCK):
                at = slice(w * BLOCK, (w + 1) * BLOCK)
                shift = top if w >= far_blocks else jnp.where(shown[w], top, -NEG)
                prob = jnp.exp2(s_g[at, :] * log2_factor - shift)
                norm = norm + jnp.sum(prob, axis=0, keepdims=True)
                s_g[at, :] = prob
            inverse = 1.0 / norm
            for w in range(width // BLOCK):
                at = slice(w * BLOCK, (w + 1) * BLOCK)
                p_all[at, lanes] = (s_g[at, :] * inverse).astype(jnp.bfloat16)
            result_t = nn(v_t[...], p_all[:, lanes])
            out_buf[h] = result_t.T.astype(jnp.bfloat16)
            grad_t = grad.astype(jnp.float32).T
            rounded = result_t.astype(jnp.bfloat16).astype(jnp.float32)
            delta = jnp.sum(grad_t * rounded, axis=0, keepdims=True)
            store_out(h).start()
            for w in range(width // BLOCK):
                at = slice(w * BLOCK, (w + 1) * BLOCK)
                ds = (s_g[at, :] * inverse) * (dp_g[at, :] - delta)
                ds_all[at, lanes] = ds.astype(jnp.bfloat16)
            dscaled = (nn(k_t[...], ds_all[:, lanes]) * factor).T
            dq_buf[h] = (dscaled * gain).astype(jnp.bfloat16)
            store_dq(h).start()
            term[pl.ds(h, 1), :] = jnp.sum(dscaled * raw, axis=0, keepdims=True)

        all_grads = g_buf[pl.ds(c * group, group)].reshape(group * rows, HD)
        for dist in range(FAR, -1, -1):
            at = slice((FAR - dist) * rows, (FAR - dist + 1) * rows)
            dkey = nn(ds_all[at, :], qs_all[...]) * factor
            dvalue = nn(p_all[at, :], all_grads)
            if dist == 0:
                part_own[c, 0] = dkey
                part_own[c, 1] = dvalue
            else:
                part_out[c, dist - 1, 0] = dkey.astype(jnp.bfloat16)
                part_out[c, dist - 1, 1] = dvalue.astype(jnp.bfloat16)

                @pl.when(me >= dist)
                def _():
                    send_part(c, dist).start()

    each(kv_count, one_kv)

    each(n_ctx, lambda i: send_ctx(i).start(), 1)

    for dist in range(1, REACH):

        @pl.when(me + dist >= n_ctx)
        def _():
            part_in[:, dist - 1] = jnp.zeros((kv_count, 2, rows, HD), jnp.bfloat16)

    def finish_kv(c):
        for dist in range(1, REACH):

            @pl.when(me + dist < n_ctx)
            def _():
                send_part(c, dist).wait_recv()

        for which in range(2):
            whole = part_own[c, which]
            for dist in range(1, REACH):
                whole = whole + part_in[c, dist - 1, which].astype(jnp.float32)
            kv_out[c, which] = whole.astype(jnp.bfloat16)
        store_dk(c).start()
        store_dv(c).start()

    each(kv_count - 1, finish_kv)

    each(n_ctx, lambda i: recv_ctx(lax.rem(me + i, n_ctx)).wait_recv(), 1)
    term_ctx[me] = term[...]
    total[...] = lax.fori_loop(
        0, n_ctx, lambda i, carry: carry + term_ctx[i], jnp.zeros(total.shape, jnp.float32)
    )
    each(n_dp, lambda i: send_dp(i).start(), 1)

    finish_kv(kv_count - 1)

    each(n_dp, lambda i: recv_dp(lax.rem(dp + i, n_dp)).wait_recv(), 1)
    total_dp[dp] = total[...]
    gain_out[...] = lax.fori_loop(
        0, n_dp, lambda i, carry: carry + total_dp[i], jnp.zeros(total.shape, jnp.float32)
    )

    each(n_ctx, lambda i: send_ctx(i).wait_send(), 1)
    each(n_dp, lambda i: send_dp(i).wait_send(), 1)

    def drain(c):
        store_dk(c).wait()
        store_dv(c).wait()
        for dist in range(1, REACH):

            @pl.when(me + dist < n_ctx)
            def _():
                send_kv(c, dist, 0).wait_send()
                send_kv(c, dist, 1).wait_send()

            @pl.when(me >= dist)
            def _():
                send_part(c, dist).wait_send()

    each(kv_count, drain)
    each(heads, lambda h: (store_out(h).wait(), store_dq(h).wait()))


def local(queries, global_keys, global_values, out_grad, query_gain, doc_start):
    rows = queries.shape[1]
    heads = queries.shape[2] // HD
    kv_count = global_keys.shape[2] // HD
    group = heads // kv_count
    width = REACH * rows
    n_dp = lax.axis_size("dp")
    n_ctx = lax.axis_size("ctx")
    begins = (jnp.repeat(doc_start[0], BLOCK) * BLOCK).reshape(1, rows)
    hbm = pl.BlockSpec(memory_space=pl.ANY)
    vmem = pl.BlockSpec(memory_space=pltpu.VMEM)
    low = jnp.bfloat16
    full = jnp.float32
    dma = pltpu.SemaphoreType.DMA
    attn_out, query_grad, key_grad, value_grad, gain_grad = pl.pallas_call(
        functools.partial(kernel, n_dp, n_ctx),
        out_shape=(
            jax.ShapeDtypeStruct(queries.shape, low),
            jax.ShapeDtypeStruct(queries.shape, low),
            jax.ShapeDtypeStruct(global_keys.shape, low),
            jax.ShapeDtypeStruct(global_keys.shape, low),
            jax.ShapeDtypeStruct((heads, HD), full),
        ),
        in_specs=[hbm, hbm, hbm, hbm, vmem, vmem],
        out_specs=(hbm, hbm, hbm, hbm, vmem),
        scratch_shapes=[
            pltpu.VMEM((heads, rows, HD), low),
            pltpu.VMEM((heads, rows, HD), low),
            pltpu.VMEM((kv_count, 2, REACH, rows, HD), low),
            pltpu.VMEM((rows, rows), full),
            pltpu.VMEM((2, width, rows), full),
            pltpu.VMEM((2, width, rows), full),
            pltpu.VMEM((width, group * rows), low),
            pltpu.VMEM((width, group * rows), low),
            pltpu.VMEM((group * rows, HD), low),
            pltpu.VMEM((HD, width), low),
            pltpu.VMEM((HD, width), low),
            pltpu.VMEM((kv_count, FAR, 2, rows, HD), low),
            pltpu.VMEM((kv_count, FAR, 2, rows, HD), low),
            pltpu.VMEM((kv_count, 2, rows, HD), full),
            pltpu.VMEM((heads, rows, HD), low),
            pltpu.VMEM((heads, rows, HD), low),
            pltpu.VMEM((kv_count, 2, rows, HD), low),
            pltpu.VMEM((heads, HD), full),
            pltpu.VMEM((n_ctx, heads, HD), full),
            pltpu.VMEM((heads, HD), full),
            pltpu.VMEM((n_dp, heads, HD), full),
            dma((2, heads)),
            dma((2, kv_count)),
            dma((kv_count, FAR, 2)),
            dma((kv_count, FAR, 2)),
            dma((kv_count, FAR)),
            dma((kv_count, FAR)),
            dma((2, heads)),
            dma((2, kv_count)),
            dma((n_ctx,)),
            dma((n_ctx,)),
            dma((n_dp,)),
            dma((n_dp,)),
        ],
        compiler_params=pltpu.CompilerParams(
            collective_id=0, has_side_effects=True, vmem_limit_bytes=48 * 1024 * 1024
        ),
    )(queries, global_keys, global_values, out_grad, query_gain.reshape(heads, HD), begins)
    return (attn_out, query_grad, key_grad, value_grad, gain_grad.reshape(-1))


def solution(mesh):
    spec = P("dp", "ctx", None)
    return jax.shard_map(
        local,
        mesh=mesh,
        in_specs=(spec, spec, spec, spec, P(), P("dp", "ctx")),
        out_specs=(spec, spec, spec, spec, P()),
        check_vma=False,
    )
```

```python
import functools
import math

import jax
import jax.numpy as jnp
from jax import lax
from jax.experimental import pallas as pl
from jax.experimental.pallas import tpu as pltpu
from jax.sharding import PartitionSpec as P

HD = 128
BLOCK = 128
REACH = 4
FAR = REACH - 1
NEG = -1e30
MESH = pl.DeviceIdType.MESH


def nt(left, right):
    return lax.dot_general(left, right, (((1,), (1,)), ((), ())), preferred_element_type=jnp.float32)


def nn(left, right):
    return jnp.dot(left, right, preferred_element_type=jnp.float32)


def kernel(
    n_dp,
    n_ctx,
    q_hbm,
    k_hbm,
    v_hbm,
    g_hbm,
    gain_ref,
    begins_ref,
    out_hbm,
    dq_hbm,
    dk_hbm,
    dv_hbm,
    gain_out,
    q_buf,
    g_buf,
    kv_buf,
    tri,
    s_buf,
    dp_buf,
    p_all,
    ds_all,
    qs_all,
    k_t,
    v_t,
    part_out,
    part_in,
    part_own,
    out_buf,
    dq_buf,
    kv_out,
    term,
    term_ctx,
    total,
    total_dp,
    load_sem,
    own_sem,
    send_sem,
    recv_sem,
    psend_sem,
    precv_sem,
    store_sem,
    kvst_sem,
    csend_sem,
    crecv_sem,
    dsend_sem,
    drecv_sem,
):
    heads, rows, _ = q_buf.shape
    kv_count = kv_buf.shape[0]
    group = heads // kv_count
    width = REACH * rows
    dp = lax.axis_index("dp")
    me = lax.axis_index("ctx")
    factor = 1.0 / math.sqrt(HD)
    log2_factor = factor * math.log2(math.e)

    def cols(index):
        return pl.ds(pl.multiple_of(index * HD, HD), HD)

    def load_q(h):
        return pltpu.make_async_copy(q_hbm.at[0, :, cols(h)], q_buf.at[h], load_sem.at[0, h])

    def load_g(h):
        return pltpu.make_async_copy(g_hbm.at[0, :, cols(h)], g_buf.at[h], load_sem.at[1, h])

    def load_k(c):
        return pltpu.make_async_copy(k_hbm.at[0, :, cols(c)], kv_buf.at[c, FAR, 0], own_sem.at[0, c])

    def load_v(c):
        return pltpu.make_async_copy(v_hbm.at[0, :, cols(c)], kv_buf.at[c, FAR, 1], own_sem.at[1, c])

    odd = lax.rem(me, 2)
    partner = me + 1 - 2 * odd

    def kv_copy(c, step, source, dist, peer):
        return pltpu.make_async_remote_copy(
            src_ref=kv_buf.at[c, source],
            dst_ref=kv_buf.at[c, FAR - dist],
            send_sem=send_sem.at[c, step],
            recv_sem=recv_sem.at[c, dist - 1],
            device_id={"ctx": peer},
            device_id_type=MESH,
        )

    def cross_kv(c):
        return kv_copy(c, 0, FAR - 2 * odd, 1, partner)

    def ahead_kv(c):
        return kv_copy(c, 1, FAR, 2, lax.rem(me + 2, n_ctx))

    def relay_kv(c):
        return kv_copy(c, 2, FAR - 1, 3, lax.rem(me + 2, n_ctx))

    def wait_kv(c, dist):
        @pl.when(me >= dist)
        def _():
            kv_copy(c, 0, FAR, dist, partner).wait_recv()

    def own_sends(c):
        load_k(c).wait()
        load_v(c).wait()

        @pl.when(odd == 0)
        def _():
            cross_kv(c).start()

        @pl.when(me + 2 < n_ctx)
        def _():
            ahead_kv(c).start()

    def relay_across(c):
        wait_kv(c, 2)

        @pl.when((odd == 1) & (me >= 2))
        def _():
            cross_kv(c).start()

    def relay_ahead(c):
        wait_kv(c, 1)

        @pl.when((me >= 1) & (me + 2 < n_ctx))
        def _():
            relay_kv(c).start()

    def part_copy(c, index, peer):
        return pltpu.make_async_remote_copy(
            src_ref=part_out.at[c, index],
            dst_ref=part_in.at[c, index],
            send_sem=psend_sem.at[c, index],
            recv_sem=precv_sem.at[c, index],
            device_id={"ctx": peer},
            device_id_type=MESH,
        )

    def cross_part(c):
        return part_copy(c, 0, partner)

    def back_part(c, index):
        return part_copy(c, index, lax.rem(me + n_ctx - 2, n_ctx))

    def add_part(c, target, source):
        for which in range(2):
            both = part_out[c, target, which].astype(jnp.float32) + part_in[
                c, source, which
            ].astype(jnp.float32)
            part_out[c, target, which] = both.astype(jnp.bfloat16)

    def parts_first(c):
        @pl.when(me >= 3)
        def _():
            back_part(c, 2).start()

        @pl.when((odd == 0) & (me >= 2))
        def _():
            back_part(c, 1).start()

    def parts_second(c):
        @pl.when((me >= 1) & (me + 2 < n_ctx))
        def _():
            back_part(c, 2).wait_recv()
            add_part(c, 0, 2)

        @pl.when(me >= 1)
        def _():
            cross_part(c).start()

    def parts_third(c):
        @pl.when((odd == 1) & (me >= 3))
        def _():
            cross_part(c).wait_recv()
            add_part(c, 1, 0)
            back_part(c, 1).start()

    def store_out(h):
        return pltpu.make_async_copy(out_buf.at[h], out_hbm.at[0, :, cols(h)], store_sem.at[0, h])

    def store_dq(h):
        return pltpu.make_async_copy(dq_buf.at[h], dq_hbm.at[0, :, cols(h)], store_sem.at[1, h])

    def store_dk(c):
        return pltpu.make_async_copy(kv_out.at[c, 0], dk_hbm.at[0, :, cols(c)], kvst_sem.at[0, c])

    def store_dv(c):
        return pltpu.make_async_copy(kv_out.at[c, 1], dv_hbm.at[0, :, cols(c)], kvst_sem.at[1, c])

    def send_ctx(step):
        return pltpu.make_async_remote_copy(
            src_ref=term,
            dst_ref=term_ctx.at[me],
            send_sem=csend_sem.at[step],
            recv_sem=crecv_sem.at[me],
            device_id={"ctx": lax.rem(me + step, n_ctx)},
            device_id_type=MESH,
        )

    def recv_ctx(peer):
        return pltpu.make_async_remote_copy(
            src_ref=term,
            dst_ref=term_ctx.at[peer],
            send_sem=csend_sem.at[0],
            recv_sem=crecv_sem.at[peer],
            device_id={"ctx": peer},
            device_id_type=MESH,
        )

    def send_dp(step):
        return pltpu.make_async_remote_copy(
            src_ref=total,
            dst_ref=total_dp.at[dp],
            send_sem=dsend_sem.at[step],
            recv_sem=drecv_sem.at[dp],
            device_id={"dp": lax.rem(dp + step, n_dp)},
            device_id_type=MESH,
        )

    def recv_dp(peer):
        return pltpu.make_async_remote_copy(
            src_ref=total,
            dst_ref=total_dp.at[peer],
            send_sem=dsend_sem.at[0],
            recv_sem=drecv_sem.at[peer],
            device_id={"dp": peer},
            device_id_type=MESH,
        )

    def each(count, body, start=0):
        def step(i, carry):
            body(i)
            return carry

        lax.fori_loop(start, count, step, 0)

    barrier = pltpu.get_barrier_semaphore()

    def greet_ctx(step):
        pl.semaphore_signal(
            barrier, inc=1, device_id={"ctx": lax.rem(me + step, n_ctx)}, device_id_type=MESH
        )

    def greet_dp(step):
        pl.semaphore_signal(
            barrier, inc=1, device_id={"dp": lax.rem(dp + step, n_dp)}, device_id_type=MESH
        )

    each(n_ctx, greet_ctx, 1)
    each(n_dp, greet_dp, 1)

    def start_loads(c):
        load_k(c).start()
        load_v(c).start()
        each(group, lambda g: (load_q(c * group + g).start(), load_g(c * group + g).start()))

    each(kv_count, start_loads)

    for dist in range(1, REACH):

        @pl.when(me < dist)
        def _():
            kv_buf[:, FAR - dist] = jnp.zeros((kv_count, 2, rows, HD), jnp.bfloat16)

    query_pos = me * rows + lax.broadcasted_iota(jnp.int32, (1, rows), 1)
    begins = begins_ref[...]
    key_pos = me * rows + lax.broadcasted_iota(jnp.int32, (rows, rows), 0)
    tri[...] = jnp.where((key_pos <= query_pos) & (key_pos >= begins), 0.0, NEG)

    pl.semaphore_wait(barrier, n_ctx - 1 + n_dp - 1)

    each(min(2, kv_count), own_sends)
    relay_across(0)
    relay_ahead(0)

    far_blocks = FAR * rows // BLOCK
    shown = []
    for w in range(far_blocks):
        first = (me - FAR) * rows + w * BLOCK
        shown.append(begins <= first)

    def exchange(c, g):
        @pl.when(c + 1 < kv_count)
        def _():
            if g == min(1, group - 1):
                relay_across(c + 1)
            if g == min(3, group - 1):
                relay_ahead(c + 1)

        @pl.when(c >= 1)
        def _():
            if g == 0:
                parts_second(c - 1)
            if g == min(2, group - 1):
                parts_third(c - 1)

    def one_kv(c):
        @pl.when(c + 2 < kv_count)
        def _():
            own_sends(c + 2)

        wait_kv(c, 3)

        keys = kv_buf[c, :, 0].reshape(width, HD)
        values = kv_buf[c, :, 1].reshape(width, HD)
        k_t[...] = keys.astype(jnp.float32).T.astype(jnp.bfloat16)
        v_t[...] = values.astype(jnp.float32).T.astype(jnp.bfloat16)

        for g in range(group):
            h = c * group + g
            lanes = pl.ds(g * rows, rows)
            s_g = s_buf.at[g % 2]
            dp_g = dp_buf.at[g % 2]
            load_q(h).wait()
            load_g(h).wait()
            gain = gain_ref[pl.ds(h, 1), :]
            raw = q_buf[h].astype(jnp.float32)
            query = (raw * gain).astype(jnp.bfloat16)
            qs_all[lanes, :] = query
            grad = g_buf[h]
            s_g[...] = nt(kv_buf[c, :, 0].reshape(width, HD), query)
            dp_g[...] = nt(kv_buf[c, :, 1].reshape(width, HD), grad)
            near = s_g[FAR * rows :, :] + tri[...]
            s_g[FAR * rows :, :] = near
            top = jnp.max(near, axis=0, keepdims=True)
            for w in range(far_blocks):
                block_top = jnp.max(s_g[w * BLOCK : (w + 1) * BLOCK, :], axis=0, keepdims=True)
                top = jnp.maximum(top, jnp.where(shown[w], block_top, NEG))
            top = top * log2_factor
            norm = jnp.zeros((1, rows), jnp.float32)
            for w in range(width // BLOCK):
                at = slice(w * BLOCK, (w + 1) * BLOCK)
                shift = top if w >= far_blocks else jnp.where(shown[w], top, -NEG)
                prob = jnp.exp2(s_g[at, :] * log2_factor - shift)
                norm = norm + jnp.sum(prob, axis=0, keepdims=True)
                s_g[at, :] = prob
            inverse = 1.0 / norm
            for w in range(width // BLOCK):
                at = slice(w * BLOCK, (w + 1) * BLOCK)
                p_all[at, lanes] = (s_g[at, :] * inverse).astype(jnp.bfloat16)
            result_t = nn(v_t[...], p_all[:, lanes])
            out_buf[h] = result_t.T.astype(jnp.bfloat16)
            grad_t = grad.astype(jnp.float32).T
            rounded = result_t.astype(jnp.bfloat16).astype(jnp.float32)
            delta = jnp.sum(grad_t * rounded, axis=0, keepdims=True)
            store_out(h).start()
            for w in range(width // BLOCK):
                at = slice(w * BLOCK, (w + 1) * BLOCK)
                ds = (s_g[at, :] * inverse) * (dp_g[at, :] - delta)
                ds_all[at, lanes] = ds.astype(jnp.bfloat16)
            dscaled = (nn(k_t[...], ds_all[:, lanes]) * factor).T
            dq_buf[h] = (dscaled * gain).astype(jnp.bfloat16)
            store_dq(h).start()
            term[pl.ds(h, 1), :] = jnp.sum(dscaled * raw, axis=0, keepdims=True)
            exchange(c, g)

        all_grads = g_buf[pl.ds(c * group, group)].reshape(group * rows, HD)
        for dist in range(FAR, -1, -1):
            at = slice((FAR - dist) * rows, (FAR - dist + 1) * rows)
            dkey = nn(ds_all[at, :], qs_all[...]) * factor
            dvalue = nn(p_all[at, :], all_grads)
            if dist == 0:
                part_own[c, 0] = dkey
                part_own[c, 1] = dvalue
            else:
                part_out[c, dist - 1, 0] = dkey.astype(jnp.bfloat16)
                part_out[c, dist - 1, 1] = dvalue.astype(jnp.bfloat16)
        parts_first(c)

    each(kv_count, one_kv)

    each(n_ctx, lambda i: send_ctx(i).start(), 1)

    last = kv_count - 1

    def finish_kv(c):
        @pl.when(me + 2 < n_ctx)
        def _():
            back_part(c, 1).wait_recv()
            for which in range(2):
                part_own[c, which] = part_own[c, which] + part_in[c, 1, which].astype(jnp.float32)

        @pl.when(odd == 0)
        def _():
            cross_part(c).wait_recv()
            for which in range(2):
                part_own[c, which] = part_own[c, which] + part_in[c, 0, which].astype(jnp.float32)

        for which in range(2):
            kv_out[c, which] = part_own[c, which].astype(jnp.bfloat16)
        store_dk(c).start()
        store_dv(c).start()

    parts_second(last)
    parts_third(last)
    each(last, finish_kv)

    each(n_ctx, lambda i: recv_ctx(lax.rem(me + i, n_ctx)).wait_recv(), 1)
    term_ctx[me] = term[...]
    total[...] = lax.fori_loop(
        0, n_ctx, lambda i, carry: carry + term_ctx[i], jnp.zeros(total.shape, jnp.float32)
    )
    each(n_dp, lambda i: send_dp(i).start(), 1)

    finish_kv(last)

    each(n_dp, lambda i: recv_dp(lax.rem(dp + i, n_dp)).wait_recv(), 1)
    total_dp[dp] = total[...]
    gain_out[...] = lax.fori_loop(
        0, n_dp, lambda i, carry: carry + total_dp[i], jnp.zeros(total.shape, jnp.float32)
    )

    each(n_ctx, lambda i: send_ctx(i).wait_send(), 1)
    each(n_dp, lambda i: send_dp(i).wait_send(), 1)

    def drain(c):
        store_dk(c).wait()
        store_dv(c).wait()

        @pl.when(me != 1)
        def _():
            cross_kv(c).wait_send()

        @pl.when(me + 2 < n_ctx)
        def _():
            ahead_kv(c).wait_send()

        @pl.when((me >= 1) & (me + 2 < n_ctx))
        def _():
            relay_kv(c).wait_send()

        @pl.when(me >= 1)
        def _():
            cross_part(c).wait_send()

        @pl.when(me >= 2)
        def _():
            back_part(c, 1).wait_send()

        @pl.when(me >= 3)
        def _():
            back_part(c, 2).wait_send()

    each(kv_count, drain)
    each(heads, lambda h: (store_out(h).wait(), store_dq(h).wait()))


PIECES = 4


def hand_on(*refs):
    count = len(refs) // 2
    sources, results, sem = refs[:count], refs[count : 2 * count], refs[-1]
    copies = []
    for index, (source, result) in enumerate(zip(sources, results)):
        rows = source.shape[1]
        pieces = PIECES if rows % (16 * PIECES) == 0 else 1
        for piece in range(pieces):
            at = pl.ds(piece * (rows // pieces), rows // pieces)
            copies.append(
                pltpu.make_async_copy(source.at[:, at], result.at[:, at], sem.at[index, piece])
            )
    for copy in copies:
        copy.start()
    for copy in copies:
        copy.wait()


def local(queries, global_keys, global_values, out_grad, query_gain, doc_start):
    rows = queries.shape[1]
    heads = queries.shape[2] // HD
    kv_count = global_keys.shape[2] // HD
    group = heads // kv_count
    width = REACH * rows
    n_dp = lax.axis_size("dp")
    n_ctx = lax.axis_size("ctx")
    begins = (jnp.repeat(doc_start[0], BLOCK) * BLOCK).reshape(1, rows)
    hbm = pl.BlockSpec(memory_space=pl.ANY)
    vmem = pl.BlockSpec(memory_space=pltpu.VMEM)
    low = jnp.bfloat16
    full = jnp.float32
    dma = pltpu.SemaphoreType.DMA
    *wide, gain_grad = pl.pallas_call(
        functools.partial(kernel, n_dp, n_ctx),
        out_shape=(
            jax.ShapeDtypeStruct(queries.shape, low),
            jax.ShapeDtypeStruct(queries.shape, low),
            jax.ShapeDtypeStruct(global_keys.shape, low),
            jax.ShapeDtypeStruct(global_keys.shape, low),
            jax.ShapeDtypeStruct((heads, HD), full),
        ),
        in_specs=[hbm, hbm, hbm, hbm, vmem, vmem],
        out_specs=(hbm, hbm, hbm, hbm, vmem),
        scratch_shapes=[
            pltpu.VMEM((heads, rows, HD), low),
            pltpu.VMEM((heads, rows, HD), low),
            pltpu.VMEM((kv_count, REACH, 2, rows, HD), low),
            pltpu.VMEM((rows, rows), full),
            pltpu.VMEM((2, width, rows), full),
            pltpu.VMEM((2, width, rows), full),
            pltpu.VMEM((width, group * rows), low),
            pltpu.VMEM((width, group * rows), low),
            pltpu.VMEM((group * rows, HD), low),
            pltpu.VMEM((HD, width), low),
            pltpu.VMEM((HD, width), low),
            pltpu.VMEM((kv_count, FAR, 2, rows, HD), low),
            pltpu.VMEM((kv_count, FAR, 2, rows, HD), low),
            pltpu.VMEM((kv_count, 2, rows, HD), full),
            pltpu.VMEM((heads, rows, HD), low),
            pltpu.VMEM((heads, rows, HD), low),
            pltpu.VMEM((kv_count, 2, rows, HD), low),
            pltpu.VMEM((heads, HD), full),
            pltpu.VMEM((n_ctx, heads, HD), full),
            pltpu.VMEM((heads, HD), full),
            pltpu.VMEM((n_dp, heads, HD), full),
            dma((2, heads)),
            dma((2, kv_count)),
            dma((kv_count, FAR)),
            dma((kv_count, FAR)),
            dma((kv_count, FAR)),
            dma((kv_count, FAR)),
            dma((2, heads)),
            dma((2, kv_count)),
            dma((n_ctx,)),
            dma((n_ctx,)),
            dma((n_dp,)),
            dma((n_dp,)),
        ],
        compiler_params=pltpu.CompilerParams(
            collective_id=0, has_side_effects=True, vmem_limit_bytes=60 * 1024 * 1024
        ),
    )(queries, global_keys, global_values, out_grad, query_gain.reshape(heads, HD), begins)
    attn_out, query_grad, key_grad, value_grad = pl.pallas_call(
        hand_on,
        out_shape=tuple(jax.ShapeDtypeStruct(item.shape, item.dtype) for item in wide),
        in_specs=[hbm] * len(wide),
        out_specs=(hbm,) * len(wide),
        scratch_shapes=[dma((len(wide), PIECES))],
        compiler_params=pltpu.CompilerParams(vmem_limit_bytes=60 * 1024 * 1024),
    )(*wide)
    return (attn_out, query_grad, key_grad, value_grad, gain_grad.reshape(-1))


def solution(mesh):
    spec = P("dp", "ctx", None)
    return jax.shard_map(
        local,
        mesh=mesh,
        in_specs=(spec, spec, spec, spec, P(), P("dp", "ctx")),
        out_specs=(spec, spec, spec, spec, P()),
        check_vma=False,
    )
```

```python
import functools
import math

import jax
import jax.numpy as jnp
from jax import lax
from jax.experimental import pallas as pl
from jax.experimental.pallas import tpu as pltpu
from jax.sharding import PartitionSpec as P

HD = 128
BLOCK = 128
REACH = 4
FAR = REACH - 1
NEG = -1e30
MESH = pl.DeviceIdType.MESH


def nt(left, right):
    return lax.dot_general(left, right, (((1,), (1,)), ((), ())), preferred_element_type=jnp.float32)


def nn(left, right):
    return jnp.dot(left, right, preferred_element_type=jnp.float32)


def kernel(
    n_dp,
    n_ctx,
    q_hbm,
    k_hbm,
    v_hbm,
    g_hbm,
    gain_ref,
    starts_ref,
    out_hbm,
    dq_hbm,
    dk_hbm,
    dv_hbm,
    gain_out,
    q_buf,
    g_buf,
    kv_buf,
    tri,
    s_buf,
    dp_buf,
    p_all,
    ds_all,
    qs_all,
    k_t,
    v_t,
    part_out,
    part_in,
    part_own,
    out_buf,
    dq_buf,
    kv_out,
    term,
    term_ctx,
    total,
    total_dp,
    load_sem,
    own_sem,
    send_sem,
    recv_sem,
    psend_sem,
    precv_sem,
    store_sem,
    kvst_sem,
    csend_sem,
    crecv_sem,
    dsend_sem,
    drecv_sem,
):
    heads, rows, _ = q_buf.shape
    kv_count = kv_buf.shape[0]
    group = heads // kv_count
    width = REACH * rows
    dp = lax.axis_index("dp")
    me = lax.axis_index("ctx")
    factor = 1.0 / math.sqrt(HD)
    log2_factor = factor * math.log2(math.e)

    def cols(index):
        return pl.ds(pl.multiple_of(index * HD, HD), HD)

    def load_q(h):
        return pltpu.make_async_copy(q_hbm.at[0, :, cols(h)], q_buf.at[h], load_sem.at[0, h])

    def load_g(h):
        return pltpu.make_async_copy(g_hbm.at[0, :, cols(h)], g_buf.at[h], load_sem.at[1, h])

    def load_k(c):
        return pltpu.make_async_copy(k_hbm.at[0, :, cols(c)], kv_buf.at[c, FAR, 0], own_sem.at[0, c])

    def load_v(c):
        return pltpu.make_async_copy(v_hbm.at[0, :, cols(c)], kv_buf.at[c, FAR, 1], own_sem.at[1, c])

    odd = lax.rem(me, 2)
    partner = me + 1 - 2 * odd

    def kv_copy(c, step, source, dist, peer):
        return pltpu.make_async_remote_copy(
            src_ref=kv_buf.at[c, source],
            dst_ref=kv_buf.at[c, FAR - dist],
            send_sem=send_sem.at[c, step],
            recv_sem=recv_sem.at[c, dist - 1],
            device_id={"ctx": peer},
            device_id_type=MESH,
        )

    def cross_kv(c):
        return kv_copy(c, 0, FAR - 2 * odd, 1, partner)

    def ahead_kv(c):
        return kv_copy(c, 1, FAR, 2, lax.rem(me + 2, n_ctx))

    def relay_kv(c):
        return kv_copy(c, 2, FAR - 1, 3, lax.rem(me + 2, n_ctx))

    def wait_kv(c, dist):
        @pl.when(me >= dist)
        def _():
            kv_copy(c, 0, FAR, dist, partner).wait_recv()

    def own_sends(c):
        load_k(c).wait()
        load_v(c).wait()

        @pl.when(odd == 0)
        def _():
            cross_kv(c).start()

        @pl.when(me + 2 < n_ctx)
        def _():
            ahead_kv(c).start()

    def relay_across(c):
        wait_kv(c, 2)

        @pl.when((odd == 1) & (me >= 2))
        def _():
            cross_kv(c).start()

    def relay_ahead(c):
        wait_kv(c, 1)

        @pl.when((me >= 1) & (me + 2 < n_ctx))
        def _():
            relay_kv(c).start()

    def part_copy(c, index, peer):
        return pltpu.make_async_remote_copy(
            src_ref=part_out.at[c, index],
            dst_ref=part_in.at[c, index],
            send_sem=psend_sem.at[c, index],
            recv_sem=precv_sem.at[c, index],
            device_id={"ctx": peer},
            device_id_type=MESH,
        )

    def cross_part(c):
        return part_copy(c, 0, partner)

    def back_part(c, index):
        return part_copy(c, index, lax.rem(me + n_ctx - 2, n_ctx))

    def add_part(c, target, source):
        for which in range(2):
            both = part_out[c, target, which].astype(jnp.float32) + part_in[
                c, source, which
            ].astype(jnp.float32)
            part_out[c, target, which] = both.astype(jnp.bfloat16)

    def parts_first(c):
        @pl.when(me >= 3)
        def _():
            back_part(c, 2).start()

        @pl.when((odd == 0) & (me >= 2))
        def _():
            back_part(c, 1).start()

    def parts_second(c):
        @pl.when((me >= 1) & (me + 2 < n_ctx))
        def _():
            back_part(c, 2).wait_recv()
            add_part(c, 0, 2)

        @pl.when(me >= 1)
        def _():
            cross_part(c).start()

    def parts_third(c):
        @pl.when((odd == 1) & (me >= 3))
        def _():
            cross_part(c).wait_recv()
            add_part(c, 1, 0)
            back_part(c, 1).start()

    def store_out(h):
        return pltpu.make_async_copy(out_buf.at[h], out_hbm.at[0, :, cols(h)], store_sem.at[0, h])

    def store_dq(h):
        return pltpu.make_async_copy(dq_buf.at[h], dq_hbm.at[0, :, cols(h)], store_sem.at[1, h])

    def store_dk(c):
        return pltpu.make_async_copy(kv_out.at[c, 0], dk_hbm.at[0, :, cols(c)], kvst_sem.at[0, c])

    def store_dv(c):
        return pltpu.make_async_copy(kv_out.at[c, 1], dv_hbm.at[0, :, cols(c)], kvst_sem.at[1, c])

    def send_ctx(step):
        return pltpu.make_async_remote_copy(
            src_ref=term,
            dst_ref=term_ctx.at[me],
            send_sem=csend_sem.at[step],
            recv_sem=crecv_sem.at[me],
            device_id={"ctx": lax.rem(me + step, n_ctx)},
            device_id_type=MESH,
        )

    def recv_ctx(peer):
        return pltpu.make_async_remote_copy(
            src_ref=term,
            dst_ref=term_ctx.at[peer],
            send_sem=csend_sem.at[0],
            recv_sem=crecv_sem.at[peer],
            device_id={"ctx": peer},
            device_id_type=MESH,
        )

    def send_dp(step):
        return pltpu.make_async_remote_copy(
            src_ref=total,
            dst_ref=total_dp.at[dp],
            send_sem=dsend_sem.at[step],
            recv_sem=drecv_sem.at[dp],
            device_id={"dp": lax.rem(dp + step, n_dp)},
            device_id_type=MESH,
        )

    def recv_dp(peer):
        return pltpu.make_async_remote_copy(
            src_ref=total,
            dst_ref=total_dp.at[peer],
            send_sem=dsend_sem.at[0],
            recv_sem=drecv_sem.at[peer],
            device_id={"dp": peer},
            device_id_type=MESH,
        )

    def each(count, body, start=0):
        def step(i, carry):
            body(i)
            return carry

        lax.fori_loop(start, count, step, 0)

    barrier = pltpu.get_barrier_semaphore()

    def greet_ctx(step):
        pl.semaphore_signal(
            barrier, inc=1, device_id={"ctx": lax.rem(me + step, n_ctx)}, device_id_type=MESH
        )

    def greet_dp(step):
        pl.semaphore_signal(
            barrier, inc=1, device_id={"dp": lax.rem(dp + step, n_dp)}, device_id_type=MESH
        )

    each(n_ctx, greet_ctx, 1)
    each(n_dp, greet_dp, 1)

    def start_loads(c):
        load_k(c).start()
        load_v(c).start()
        each(group, lambda g: (load_q(c * group + g).start(), load_g(c * group + g).start()))

    each(kv_count, start_loads)

    for dist in range(1, REACH):

        @pl.when(me < dist)
        def _():
            kv_buf[:, FAR - dist] = jnp.zeros((kv_count, 2, rows, HD), jnp.bfloat16)

    query_pos = me * rows + lax.broadcasted_iota(jnp.int32, (1, rows), 1)
    lane_block = lax.broadcasted_iota(jnp.int32, (1, rows), 1) // BLOCK
    begins = jnp.zeros((1, rows), jnp.int32)
    for b in range(rows // BLOCK):
        begins = jnp.where(lane_block == b, starts_ref[0, b] * BLOCK, begins)
    key_pos = me * rows + lax.broadcasted_iota(jnp.int32, (rows, rows), 0)
    tri[...] = jnp.where((key_pos <= query_pos) & (key_pos >= begins), 0.0, NEG)

    pl.semaphore_wait(barrier, n_ctx - 1 + n_dp - 1)

    each(min(2, kv_count), own_sends)
    relay_across(0)
    relay_ahead(0)

    far_blocks = FAR * rows // BLOCK
    shown = []
    for w in range(far_blocks):
        first = (me - FAR) * rows + w * BLOCK
        shown.append(begins <= first)

    def exchange(c, g):
        @pl.when(c + 1 < kv_count)
        def _():
            if g == min(1, group - 1):
                relay_across(c + 1)
            if g == min(3, group - 1):
                relay_ahead(c + 1)

        @pl.when(c >= 1)
        def _():
            if g == 0:
                parts_second(c - 1)
            if g == min(2, group - 1):
                parts_third(c - 1)

    def one_kv(c):
        @pl.when(c + 2 < kv_count)
        def _():
            own_sends(c + 2)

        wait_kv(c, 3)

        keys = kv_buf[c, :, 0].reshape(width, HD)
        values = kv_buf[c, :, 1].reshape(width, HD)
        k_t[...] = keys.astype(jnp.float32).T.astype(jnp.bfloat16)
        v_t[...] = values.astype(jnp.float32).T.astype(jnp.bfloat16)

        for g in range(group):
            h = c * group + g
            lanes = pl.ds(g * rows, rows)
            s_g = s_buf.at[g % 2]
            dp_g = dp_buf.at[g % 2]
            load_q(h).wait()
            load_g(h).wait()
            gain = gain_ref[pl.ds(h, 1), :]
            raw = q_buf[h].astype(jnp.float32)
            query = (raw * gain).astype(jnp.bfloat16)
            qs_all[lanes, :] = query
            grad = g_buf[h]
            s_g[...] = nt(kv_buf[c, :, 0].reshape(width, HD), query)
            dp_g[...] = nt(kv_buf[c, :, 1].reshape(width, HD), grad)
            near = s_g[FAR * rows :, :] + tri[...]
            s_g[FAR * rows :, :] = near
            top = jnp.max(near, axis=0, keepdims=True)
            for w in range(far_blocks):
                block_top = jnp.max(s_g[w * BLOCK : (w + 1) * BLOCK, :], axis=0, keepdims=True)
                top = jnp.maximum(top, jnp.where(shown[w], block_top, NEG))
            top = top * log2_factor
            norm = jnp.zeros((1, rows), jnp.float32)
            for w in range(width // BLOCK):
                at = slice(w * BLOCK, (w + 1) * BLOCK)
                shift = top if w >= far_blocks else jnp.where(shown[w], top, -NEG)
                prob = jnp.exp2(s_g[at, :] * log2_factor - shift)
                norm = norm + jnp.sum(prob, axis=0, keepdims=True)
                s_g[at, :] = prob
            inverse = 1.0 / norm
            for w in range(width // BLOCK):
                at = slice(w * BLOCK, (w + 1) * BLOCK)
                p_all[at, lanes] = (s_g[at, :] * inverse).astype(jnp.bfloat16)
            result_t = nn(v_t[...], p_all[:, lanes])
            out_buf[h] = result_t.T.astype(jnp.bfloat16)
            grad_t = grad.astype(jnp.float32).T
            rounded = result_t.astype(jnp.bfloat16).astype(jnp.float32)
            delta = jnp.sum(grad_t * rounded, axis=0, keepdims=True)
            store_out(h).start()
            for w in range(width // BLOCK):
                at = slice(w * BLOCK, (w + 1) * BLOCK)
                ds = (s_g[at, :] * inverse) * (dp_g[at, :] - delta)
                ds_all[at, lanes] = ds.astype(jnp.bfloat16)
            dscaled = (nn(k_t[...], ds_all[:, lanes]) * factor).T
            dq_buf[h] = (dscaled * gain).astype(jnp.bfloat16)
            store_dq(h).start()
            term[pl.ds(h, 1), :] = jnp.sum(dscaled * raw, axis=0, keepdims=True)
            exchange(c, g)

        all_grads = g_buf[pl.ds(c * group, group)].reshape(group * rows, HD)
        for dist in range(FAR, -1, -1):
            at = slice((FAR - dist) * rows, (FAR - dist + 1) * rows)
            dkey = nn(ds_all[at, :], qs_all[...]) * factor
            dvalue = nn(p_all[at, :], all_grads)
            if dist == 0:
                part_own[c, 0] = dkey
                part_own[c, 1] = dvalue
            else:
                part_out[c, dist - 1, 0] = dkey.astype(jnp.bfloat16)
                part_out[c, dist - 1, 1] = dvalue.astype(jnp.bfloat16)
        parts_first(c)

    each(kv_count, one_kv)

    each(n_ctx, lambda i: send_ctx(i).start(), 1)

    last = kv_count - 1

    def finish_kv(c):
        @pl.when(me + 2 < n_ctx)
        def _():
            back_part(c, 1).wait_recv()
            for which in range(2):
                part_own[c, which] = part_own[c, which] + part_in[c, 1, which].astype(jnp.float32)

        @pl.when(odd == 0)
        def _():
            cross_part(c).wait_recv()
            for which in range(2):
                part_own[c, which] = part_own[c, which] + part_in[c, 0, which].astype(jnp.float32)

        for which in range(2):
            kv_out[c, which] = part_own[c, which].astype(jnp.bfloat16)
        store_dk(c).start()
        store_dv(c).start()

    parts_second(last)
    parts_third(last)
    each(last, finish_kv)

    each(n_ctx, lambda i: recv_ctx(lax.rem(me + i, n_ctx)).wait_recv(), 1)
    term_ctx[me] = term[...]
    total[...] = lax.fori_loop(
        0, n_ctx, lambda i, carry: carry + term_ctx[i], jnp.zeros(total.shape, jnp.float32)
    )
    each(n_dp, lambda i: send_dp(i).start(), 1)

    finish_kv(last)

    each(n_dp, lambda i: recv_dp(lax.rem(dp + i, n_dp)).wait_recv(), 1)
    total_dp[dp] = total[...]
    gain_out[...] = lax.fori_loop(
        0, n_dp, lambda i, carry: carry + total_dp[i], jnp.zeros(total.shape, jnp.float32)
    )

    each(n_ctx, lambda i: send_ctx(i).wait_send(), 1)
    each(n_dp, lambda i: send_dp(i).wait_send(), 1)

    def drain(c):
        store_dk(c).wait()
        store_dv(c).wait()

        @pl.when(me != 1)
        def _():
            cross_kv(c).wait_send()

        @pl.when(me + 2 < n_ctx)
        def _():
            ahead_kv(c).wait_send()

        @pl.when((me >= 1) & (me + 2 < n_ctx))
        def _():
            relay_kv(c).wait_send()

        @pl.when(me >= 1)
        def _():
            cross_part(c).wait_send()

        @pl.when(me >= 2)
        def _():
            back_part(c, 1).wait_send()

        @pl.when(me >= 3)
        def _():
            back_part(c, 2).wait_send()

    each(kv_count, drain)
    each(heads, lambda h: (store_out(h).wait(), store_dq(h).wait()))


PIECES = 4


def hand_on(*refs):
    count = len(refs) // 2
    for source, result in zip(refs[:count], refs[count:]):
        result[...] = source[...]


def local(queries, global_keys, global_values, out_grad, query_gain, doc_start):
    rows = queries.shape[1]
    heads = queries.shape[2] // HD
    kv_count = global_keys.shape[2] // HD
    group = heads // kv_count
    width = REACH * rows
    n_dp = lax.axis_size("dp")
    n_ctx = lax.axis_size("ctx")
    hbm = pl.BlockSpec(memory_space=pl.ANY)
    vmem = pl.BlockSpec(memory_space=pltpu.VMEM)
    low = jnp.bfloat16
    full = jnp.float32
    dma = pltpu.SemaphoreType.DMA
    *wide, gain_grad = pl.pallas_call(
        functools.partial(kernel, n_dp, n_ctx),
        out_shape=(
            jax.ShapeDtypeStruct(queries.shape, low),
            jax.ShapeDtypeStruct(queries.shape, low),
            jax.ShapeDtypeStruct(global_keys.shape, low),
            jax.ShapeDtypeStruct(global_keys.shape, low),
            jax.ShapeDtypeStruct((heads, HD), full),
        ),
        in_specs=[hbm, hbm, hbm, hbm, vmem, pl.BlockSpec(memory_space=pltpu.SMEM)],
        out_specs=(hbm, hbm, hbm, hbm, vmem),
        scratch_shapes=[
            pltpu.VMEM((heads, rows, HD), low),
            pltpu.VMEM((heads, rows, HD), low),
            pltpu.VMEM((kv_count, REACH, 2, rows, HD), low),
            pltpu.VMEM((rows, rows), full),
            pltpu.VMEM((2, width, rows), full),
            pltpu.VMEM((2, width, rows), full),
            pltpu.VMEM((width, group * rows), low),
            pltpu.VMEM((width, group * rows), low),
            pltpu.VMEM((group * rows, HD), low),
            pltpu.VMEM((HD, width), low),
            pltpu.VMEM((HD, width), low),
            pltpu.VMEM((kv_count, FAR, 2, rows, HD), low),
            pltpu.VMEM((kv_count, FAR, 2, rows, HD), low),
            pltpu.VMEM((kv_count, 2, rows, HD), full),
            pltpu.VMEM((heads, rows, HD), low),
            pltpu.VMEM((heads, rows, HD), low),
            pltpu.VMEM((kv_count, 2, rows, HD), low),
            pltpu.VMEM((heads, HD), full),
            pltpu.VMEM((n_ctx, heads, HD), full),
            pltpu.VMEM((heads, HD), full),
            pltpu.VMEM((n_dp, heads, HD), full),
            dma((2, heads)),
            dma((2, kv_count)),
            dma((kv_count, FAR)),
            dma((kv_count, FAR)),
            dma((kv_count, FAR)),
            dma((kv_count, FAR)),
            dma((2, heads)),
            dma((2, kv_count)),
            dma((n_ctx,)),
            dma((n_ctx,)),
            dma((n_dp,)),
            dma((n_dp,)),
        ],
        compiler_params=pltpu.CompilerParams(
            collective_id=0, has_side_effects=True, vmem_limit_bytes=60 * 1024 * 1024
        ),
    )(queries, global_keys, global_values, out_grad, query_gain.reshape(heads, HD), doc_start)
    pieces = PIECES if rows % (16 * PIECES) == 0 else 1
    blocks = [
        pl.BlockSpec((1, rows // pieces, item.shape[2]), lambda i: (0, i, 0)) for item in wide
    ]
    attn_out, query_grad, key_grad, value_grad = pl.pallas_call(
        hand_on,
        grid=(pieces,),
        out_shape=tuple(jax.ShapeDtypeStruct(item.shape, item.dtype) for item in wide),
        in_specs=blocks,
        out_specs=tuple(blocks),
        compiler_params=pltpu.CompilerParams(vmem_limit_bytes=60 * 1024 * 1024),
    )(*wide)
    return (attn_out, query_grad, key_grad, value_grad, gain_grad.reshape(-1))


def solution(mesh):
    spec = P("dp", "ctx", None)
    return jax.shard_map(
        local,
        mesh=mesh,
        in_specs=(spec, spec, spec, spec, P(), P("dp", "ctx")),
        out_specs=(spec, spec, spec, spec, P()),
        check_vma=False,
    )
```
